512 devices in a mesh: section: 4 (over y_hi, core), dp: 8 (over z), tensor: 16 (over x, y_lo).
Axes of the slice: x: 4, y: 8 (y_hi: 2, y_lo: 4; y = y_hi * 4 + y_lo), z: 8, core: 2. Of those that a mesh axis runs over, the one named last changes fastest.
Arguments:
- saved_input: bfloat16 [4, 256, 8192], P('section', 'dp', 'tensor'), may hold values from -6 to 6
- w_up: bfloat16 [4, 8192, 16384], P('section', 'tensor', 'dp'), may hold values from -0.0625 to 0.0625
- w_down: bfloat16 [4, 16384, 8192], P('section', 'dp', 'tensor'), may hold values from -0.046875 to 0.046875
- sent_grad: bfloat16 [4, 256, 8192], P('section', ('dp', 'tensor')), may hold values from -6 to 6
Outputs:
- input_grad: bfloat16 [4, 256, 8192], P('section', 'dp', 'tensor')
The draws below stay inside these ranges and needn't reach their ends.
All inputs are finite; a program needn't handle non-finite values.
Results may differ from the reference program's by a relative error of at most 0.02.
Values may be sent and summed in bfloat16 or wider, within the bound.
No kernel may reach another device: no remote copies, remote signals or barrier semaphores. Data moves between devices by JAX's collectives and lax.ppermute only.
A program may use at most 64 MiB of HBM per device.

```python
import jax
import jax.numpy as jnp
from jax import lax

D = 8192
FF = 16384
TOKENS = 256
SECTIONS = 4
N_SECTION = 4
N_TENSOR = 16


def block_levels(stream_key, extent, shards, least, largest):
    factor_of, own = 1.0, jax.random.fold_in(stream_key, 6)
    for position, parts in shards:
        draws = jnp.exp(jax.random.uniform(jax.random.fold_in(own, position), (parts,), jnp.float32, least / len(shards), largest / len(shards)))
        factor_of = factor_of * jnp.repeat(draws, extent[position] // parts).reshape([-1 if axis == position else 1 for axis in range(len(extent))])
    return factor_of


def centred(stream_key, dims, deviation, reach, split=(), kind=jnp.bfloat16):
    drawn = jax.random.normal(stream_key, dims, jnp.float32) * deviation
    if len(split) > 0:
        drawn = block_levels(stream_key, dims, split, -0.22, 0.18) * drawn
    return jnp.clip(drawn, min=-reach, max=reach).astype(kind)


def setup_inputs(seed: int = 0) -> dict:
    key_list = jax.random.split(jax.random.key(seed), 5)
    return {
        "saved_input": centred(key_list[0], (SECTIONS, TOKENS, D), 1.0, 6.0, ((0, 4), (1, 8), (2, 16))),
        "w_up": centred(key_list[1], (SECTIONS, D, FF), D ** -0.5, 0.0625, ((0, 4), (1, 16), (2, 8))),
        "w_down": centred(key_list[2], (SECTIONS, FF, D), FF ** -0.5, 0.046875, ((0, 4), (1, 8), (2, 16))),
        "sent_grad": centred(key_list[3], (SECTIONS, TOKENS, D), 1.0, 6.0, ((0, 4), (1, 128))),
    }


def gelu_slope(value):
    coeff = 0.7978845608028654
    inner = coeff * (value + 0.044715 * value * value * value)
    tangent = jnp.tanh(inner)
    return 0.5 * (1.0 + tangent) + 0.5 * value * (1.0 - tangent * tangent) * coeff * (1.0 + 3.0 * 0.044715 * value * value)


def one_section(tokens_in, up_weight, down_weight, grad_out):
    block = D // N_TENSOR
    total_rows = tokens_in.shape[0]

    def add_block(carry, index):
        begin = (index * block).astype(jnp.int32)
        feat_in = lax.dynamic_slice_in_dim(tokens_in, begin, block, 1)
        up_rows = lax.dynamic_slice_in_dim(up_weight, begin, block, 0)
        grad_cols = lax.dynamic_slice_in_dim(grad_out, begin, block, 1)
        down_cols = lax.dynamic_slice_in_dim(down_weight, begin, block, 1)
        hid_part = jnp.dot(feat_in, up_rows, preferred_element_type=jnp.float32).astype(jnp.bfloat16)
        back_part = lax.dot_general(grad_cols, down_cols, (((1,), (1,)), ((), ())), preferred_element_type=jnp.float32).astype(jnp.bfloat16)
        hid_part, back_part = lax.optimization_barrier((hid_part, back_part))
        return (carry[0] + hid_part.astype(jnp.float32), carry[1] + back_part.astype(jnp.float32)), None

    zeros = jnp.zeros((total_rows, up_weight.shape[1]), jnp.float32)
    (hidden, back_hidden), _ = lax.scan(add_block, (zeros, zeros), jnp.arange(N_TENSOR, dtype=jnp.int32))
    slope_grad = (back_hidden * gelu_slope(hidden)).astype(jnp.bfloat16)
    branch = lax.dot_general(slope_grad, up_weight, (((1,), (1,)), ((), ())), preferred_element_type=jnp.float32)
    return (grad_out.astype(jnp.float32) + branch).astype(jnp.bfloat16)


def reference(saved_input, w_up, w_down, sent_grad):
    out_grad = jnp.roll(sent_grad, -1, axis=0)
    results = []
    for section_index in range(N_SECTION):
        results.append(one_section(saved_input[section_index], w_up[section_index], w_down[section_index], out_grad[section_index]))
    return jnp.stack(results, axis=0)
```

```python
import jax
import jax.numpy as jnp
from jax import lax
from jax.sharding import Mesh
from jax.sharding import PartitionSpec as P

TENSOR = ("tx", "ty")


def shifted(value, axis, steps):
    count = lax.axis_size(axis)
    pairs = [(source, (source + steps) % count) for source in range(count)]
    return lax.ppermute(value, axis, pairs)


def gathered(value, axis):
    count = lax.axis_size(axis)
    copies = jnp.broadcast_to(value[None], (count,) + value.shape)
    parts = lax.all_to_all(copies, axis, split_axis=0, concat_axis=0, tiled=True)
    return parts.reshape((count * value.shape[0],) + value.shape[1:])


def scattered_sum(value, axis):
    count = lax.axis_size(axis)
    split = value.reshape((count, value.shape[0] // count) + value.shape[1:])
    parts = lax.all_to_all(split, axis, split_axis=0, concat_axis=0, tiled=True)
    return jnp.sum(parts.astype(jnp.float32), axis=0)


def tensor_sum(part):
    across_x = scattered_sum(part.astype(jnp.bfloat16), "tx")
    return scattered_sum(across_x.astype(jnp.bfloat16), "ty")


def gelu_slope(value):
    coeff = 0.7978845608028654
    inner = coeff * (value + 0.044715 * value * value * value)
    tangent = jnp.tanh(inner)
    return 0.5 * (1.0 + tangent) + 0.5 * value * (1.0 - tangent * tangent) * coeff * (
        1.0 + 3.0 * 0.044715 * value * value
    )


def per_device(saved_input, w_up, w_down, sent_grad):
    tokens_in = saved_input[0]
    up_block = w_up[0]
    down_block = w_down[0]
    contract_last = (((1,), (1,)), ((), ()))
    moved = shifted(sent_grad[0], "section", -1)
    local_grad = lax.all_to_all(moved, TENSOR, split_axis=1, concat_axis=0, tiled=True)
    hidden_part = jnp.dot(
        gathered(tokens_in, "dp"), up_block, preferred_element_type=jnp.float32
    )
    hidden = tensor_sum(hidden_part)
    back_part = lax.dot_general(
        gathered(local_grad, "dp"),
        down_block,
        contract_last,
        preferred_element_type=jnp.float32,
    )
    back_hidden = tensor_sum(back_part)
    slope_grad = (back_hidden * gelu_slope(hidden)).astype(jnp.bfloat16)
    slope_grad = gathered(gathered(slope_grad, "ty"), "tx")
    branch = lax.dot_general(
        slope_grad, up_block, contract_last, preferred_element_type=jnp.float32
    )
    summed = scattered_sum(branch.astype(jnp.bfloat16), "dp")
    result = (local_grad.astype(jnp.float32) + summed).astype(jnp.bfloat16)
    return result[None]


def solution(mesh):
    count_y = 4
    sizes = (
        mesh.shape["section"],
        mesh.shape["dp"],
        mesh.shape["tensor"] // count_y,
        count_y,
    )
    fine = Mesh(mesh.devices.reshape(sizes), ("section", "dp") + TENSOR)
    in_specs = (
        P("section", "dp", TENSOR),
        P("section", TENSOR, "dp"),
        P("section", "dp", TENSOR),
        P("section", ("dp",) + TENSOR, None),
    )
    out_specs = P("section", "dp", TENSOR)
    return jax.shard_map(
        per_device, mesh=fine, in_specs=in_specs, out_specs=out_specs, check_vma=False
    )
```

```python
import jax
import jax.numpy as jnp
from jax import lax
from jax.sharding import Mesh
from jax.sharding import PartitionSpec as P

TENSOR = ("tx", "ty1", "ty0")
NEAR = ("tx", "ty0")


def exchange(value, axis):
    return lax.all_to_all(value, axis, split_axis=0, concat_axis=0, tiled=True)


def copies(value, axis):
    return jnp.broadcast_to(value[None], (lax.axis_size(axis),) + value.shape)


def gelu_slope(value):
    coeff = 0.7978845608028654
    inner = coeff * (value + 0.044715 * value * value * value)
    tangent = jnp.tanh(inner)
    return 0.5 * (1.0 + tangent) + 0.5 * value * (1.0 - tangent * tangent) * coeff * (
        1.0 + 3.0 * 0.044715 * value * value
    )


def previous_section_grad(sent):
    sections, parts = lax.axis_size("section"), lax.axis_size(TENSOR)
    tokens, width = sent.shape
    here = lax.axis_index("section")
    blocks = sent.reshape(tokens, parts, width // parts).transpose(1, 0, 2)
    slots = lax.broadcasted_iota(jnp.int32, (sections, 1, 1, 1), 0)
    blocks = jnp.where(slots == (here + sections - 1) % sections, blocks[None], 0)
    blocks = blocks.reshape((sections * parts,) + blocks.shape[2:])
    blocks = exchange(blocks, ("section",) + TENSOR)
    blocks = blocks.reshape(sections, parts * tokens, width // parts)
    return lax.dynamic_index_in_dim(
        blocks, (here + 1) % sections, axis=0, keepdims=False
    )


def per_device(saved_input, w_up, w_down, sent_grad):
    tokens_in = saved_input[0]
    up_block = w_up[0]
    down_block = w_down[0]
    rows, width = tokens_in.shape
    up_turned, down_turned = lax.optimization_barrier((up_block.T, down_block.T))
    local_grad = previous_section_grad(sent_grad[0])
    pair = jnp.concatenate([tokens_in, local_grad], axis=1)
    pair = exchange(copies(pair, "dp"), "dp").reshape(-1, 2 * width)
    hidden_part = jnp.dot(
        pair[:, :width], up_block, preferred_element_type=jnp.float32
    ).astype(jnp.bfloat16)
    back_part = jnp.dot(
        pair[:, width:], down_turned, preferred_element_type=jnp.float32
    ).astype(jnp.bfloat16)
    near = lax.axis_size(NEAR)
    units = hidden_part.shape[1]
    parts = jnp.stack(
        [hidden_part.reshape(near, -1, units), back_part.reshape(near, -1, units)],
        axis=1,
    )
    near_sum = jnp.sum(exchange(parts, NEAR).astype(jnp.float32), axis=0)
    near_sum = near_sum.astype(jnp.bfloat16)
    far_sum = lax.ppermute(near_sum, "ty1", [(0, 1), (1, 0)])
    sums = near_sum.astype(jnp.float32) + far_sum.astype(jnp.float32)
    slope_grad = (sums[1] * gelu_slope(sums[0])).astype(jnp.bfloat16)
    slope_grad = exchange(copies(slope_grad, NEAR), NEAR).reshape(-1, units)
    branch = jnp.dot(slope_grad, up_turned, preferred_element_type=jnp.float32)
    branch = branch.astype(jnp.bfloat16).reshape(-1, rows, width)
    summed = jnp.sum(exchange(branch, "dp").astype(jnp.float32), axis=0)
    result = (local_grad.astype(jnp.float32) + summed).astype(jnp.bfloat16)
    return result[None]


def solution(mesh):
    sections, dp, tensor = (mesh.shape[a] for a in ("section", "dp", "tensor"))
    fine = Mesh(
        mesh.devices.reshape(sections, dp, tensor // 4, 2, 2),
        ("section", "dp") + TENSOR,
    )
    in_specs = (
        P("section", "dp", TENSOR),
        P("section", TENSOR, "dp"),
        P("section", "dp", TENSOR),
        P("section", ("dp",) + TENSOR, None),
    )
    out_specs = P("section", "dp", TENSOR)
    return jax.shard_map(
        per_device, mesh=fine, in_specs=in_specs, out_specs=out_specs, check_vma=False
    )
```

```python
import jax
import jax.numpy as jnp
from jax import lax
from jax.sharding import Mesh
from jax.sharding import PartitionSpec as P

TENSOR = ("tx", "ty1", "ty0")
NEAR = ("tx", "ty0")


def exchange(value, axis):
    return lax.all_to_all(value, axis, split_axis=0, concat_axis=0, tiled=True)


def copies(value, axis):
    return jnp.broadcast_to(value[None], (lax.axis_size(axis),) + value.shape)


def shifted(value, axis, steps):
    count = lax.axis_size(axis)
    pairs = [(source, (source + steps) % count) for source in range(count)]
    return lax.ppermute(value, axis, pairs)


def gelu_slope(value):
    coeff = 0.7978845608028654
    inner = coeff * (value + 0.044715 * value * value * value)
    tangent = jnp.tanh(inner)
    return 0.5 * (1.0 + tangent) + 0.5 * value * (1.0 - tangent * tangent) * coeff * (
        1.0 + 3.0 * 0.044715 * value * value
    )


def block_sum(blocks):
    return sum(block.astype(jnp.float32) for block in blocks)


def permuted_blocks(part, axis):
    count, here = lax.axis_size(axis), lax.axis_index(axis)
    blocks = part.reshape((count, part.shape[0] // count) + part.shape[1:])

    def block(steps):
        return lax.dynamic_index_in_dim(
            blocks, (here + steps) % count, axis=0, keepdims=False
        )

    return [block(0)] + [
        shifted(block(steps), axis, steps) for steps in range(1, count)
    ]


def per_device(saved_input, w_up, w_down, sent_grad):
    tokens_in = saved_input[0]
    up_block = w_up[0]
    down_block = w_down[0]
    rows, width = tokens_in.shape
    near = lax.axis_size(NEAR)
    sent = sent_grad[0]
    parts = lax.axis_size(TENSOR)

    up_turned, down_turned = lax.optimization_barrier((up_block.T, down_block.T))
    moved = shifted(sent, "section", -1)
    all_tokens = exchange(copies(tokens_in, "dp"), "dp").reshape(-1, width)
    hidden_part = jnp.dot(
        all_tokens, up_block, preferred_element_type=jnp.float32
    ).astype(jnp.bfloat16)
    units = hidden_part.shape[1]

    hidden_part, moved = lax.optimization_barrier((hidden_part, moved))
    moved = moved.reshape(-1, parts, width).transpose(1, 0, 2)
    local_grad = exchange(moved, TENSOR).reshape(rows, width)
    hidden = block_sum(permuted_blocks(hidden_part, "tx")).astype(jnp.bfloat16)
    local_grad, hidden = lax.optimization_barrier((local_grad, hidden))
    all_grads = exchange(copies(local_grad, "dp"), "dp").reshape(-1, width)
    hidden = block_sum(permuted_blocks(hidden, "ty0")).astype(jnp.bfloat16)
    back_part = jnp.dot(
        all_grads, down_turned, preferred_element_type=jnp.float32
    ).astype(jnp.bfloat16)
    back_part, hidden = lax.optimization_barrier((back_part, hidden))
    back_near = jnp.sum(
        exchange(back_part.reshape(near, -1, units), NEAR).astype(jnp.float32), axis=0
    ).astype(jnp.bfloat16)
    slope = gelu_slope(block_sum([hidden, shifted(hidden, "ty1", 1)]))
    back_near, slope = lax.optimization_barrier((back_near, slope))
    back_far = shifted(back_near, "ty1", 1)
    back_hidden = back_near.astype(jnp.float32) + back_far.astype(jnp.float32)
    slope_grad = (back_hidden * slope).astype(jnp.bfloat16)
    slope_grad = exchange(copies(slope_grad, NEAR), NEAR).reshape(-1, units)
    branch = jnp.dot(slope_grad, up_turned, preferred_element_type=jnp.float32)
    branch = branch.astype(jnp.bfloat16).reshape(-1, rows, width)
    summed = jnp.sum(exchange(branch, "dp").astype(jnp.float32), axis=0)
    result = (local_grad.astype(jnp.float32) + summed).astype(jnp.bfloat16)
    return result[None]


def solution(mesh):
    sections, dp, tensor = (mesh.shape[a] for a in ("section", "dp", "tensor"))
    fine = Mesh(
        mesh.devices.reshape(sections, dp, tensor // 4, 2, 2),
        ("section", "dp") + TENSOR,
    )
    in_specs = (
        P("section", "dp", TENSOR),
        P("section", TENSOR, "dp"),
        P("section", "dp", TENSOR),
        P("section", ("dp",) + TENSOR, None),
    )
    out_specs = P("section", "dp", TENSOR)
    return jax.shard_map(
        per_device, mesh=fine, in_specs=in_specs, out_specs=out_specs, check_vma=False
    )
```

```python
import jax
import jax.numpy as jnp
from jax import lax
from jax.experimental import pallas as pl
from jax.experimental.pallas import tpu as pltpu
from jax.sharding import Mesh
from jax.sharding import PartitionSpec as P

LONG = pl.CostEstimate(flops=2 * 10**10, bytes_accessed=2**20, transcendentals=0)
TENSOR = ("tx", "ty1", "ty0")
NEAR = ("tx", "ty0")


def exchange(value, axis):
    return lax.all_to_all(value, axis, split_axis=0, concat_axis=0, tiled=True)


def copies(value, axis):
    return jnp.broadcast_to(value[None], (lax.axis_size(axis),) + value.shape)


def shifted(value, axis, steps):
    count = lax.axis_size(axis)
    pairs = [(source, (source + steps) % count) for source in range(count)]
    return lax.ppermute(value, axis, pairs)


def gelu_slope(value):
    coeff = 0.7978845608028654
    inner = coeff * (value + 0.044715 * value * value * value)
    tangent = jnp.tanh(inner)
    return 0.5 * (1.0 + tangent) + 0.5 * value * (1.0 - tangent * tangent) * coeff * (
        1.0 + 3.0 * 0.044715 * value * value
    )


def block_sum(blocks):
    return sum(block.astype(jnp.float32) for block in blocks)


def permuted_blocks(part, axis):
    count, here = lax.axis_size(axis), lax.axis_index(axis)
    blocks = part.reshape((count, part.shape[0] // count) + part.shape[1:])

    def block(steps):
        return lax.dynamic_index_in_dim(
            blocks, (here + steps) % count, axis=0, keepdims=False
        )

    return [block(0)] + [
        shifted(block(steps), axis, steps) for steps in range(1, count)
    ]


def copies_kernel(value_ref, copies_ref, sems):
    moves = [
        pltpu.make_async_copy(value_ref, copies_ref.at[at], sems.at[at])
        for at in range(copies_ref.shape[0])
    ]
    for move in moves:
        move.start()
    for move in moves:
        move.wait()


def long_copies(value, axis):
    count = lax.axis_size(axis)
    return pl.pallas_call(
        copies_kernel,
        out_shape=jax.ShapeDtypeStruct((count,) + value.shape, value.dtype),
        in_specs=[pl.BlockSpec(memory_space=pl.ANY)],
        out_specs=pl.BlockSpec(memory_space=pltpu.HBM),
        scratch_shapes=[pltpu.SemaphoreType.DMA((count,))],
        compiler_params=pltpu.CompilerParams(vmem_limit_bytes=2**20),
        cost_estimate=LONG,
    )(value)


def turned_dot_kernel(left_ref, right_ref, out_ref):
    step = 512
    for begin in range(0, out_ref.shape[1], step):
        out_ref[:, begin : begin + step] = lax.dot_general(
            left_ref[...],
            right_ref[begin : begin + step, :],
            (((1,), (1,)), ((), ())),
            preferred_element_type=jnp.float32,
        ).astype(out_ref.dtype)


def turned_dot(left, right):
    rows, units = left.shape[0], right.shape[0]
    vmem = pl.BlockSpec(memory_space=pltpu.VMEM)
    return pl.pallas_call(
        turned_dot_kernel,
        out_shape=jax.ShapeDtypeStruct((rows, units), jnp.bfloat16),
        in_specs=[vmem, vmem],
        out_specs=vmem,
        compiler_params=pltpu.CompilerParams(vmem_limit_bytes=8 * 2**20),
        cost_estimate=LONG,
    )(left, pltpu.with_memory_space_constraint(right, pltpu.VMEM))


def per_device(saved_input, w_up, w_down, sent_grad):
    tokens_in = saved_input[0]
    up_block = w_up[0]
    down_block = w_down[0]
    rows, width = tokens_in.shape
    near = lax.axis_size(NEAR)
    sent = sent_grad[0]
    parts = lax.axis_size(TENSOR)

    moved = shifted(sent, "section", -1)
    all_tokens = exchange(copies(tokens_in, "dp"), "dp").reshape(-1, width)
    hidden_part = jnp.dot(
        all_tokens, up_block, preferred_element_type=jnp.float32
    ).astype(jnp.bfloat16)
    units = hidden_part.shape[1]

    hidden_part, moved = lax.optimization_barrier((hidden_part, moved))
    moved = moved.reshape(-1, parts, width).transpose(1, 0, 2)
    local_grad = exchange(moved, TENSOR).reshape(rows, width)
    (local_grad,) = lax.optimization_barrier((local_grad,))
    hidden = block_sum(permuted_blocks(hidden_part, "tx")).astype(jnp.bfloat16)
    all_grads = exchange(long_copies(local_grad, "dp"), "dp").reshape(-1, width)
    arrived = permuted_blocks(hidden, "ty0")
    back_part = turned_dot(all_grads, down_block)
    back_part, arrived = lax.optimization_barrier((back_part, arrived))
    hidden = block_sum(arrived).astype(jnp.bfloat16)
    back_near = jnp.sum(
        exchange(back_part.reshape(near, -1, units), NEAR).astype(jnp.float32), axis=0
    ).astype(jnp.bfloat16)
    slope = gelu_slope(block_sum([hidden, shifted(hidden, "ty1", 1)]))
    back_near, slope = lax.optimization_barrier((back_near, slope))
    back_far = shifted(back_near, "ty1", 1)
    back_hidden = back_near.astype(jnp.float32) + back_far.astype(jnp.float32)
    slope_grad = (back_hidden * slope).astype(jnp.bfloat16)
    slope_grad = exchange(copies(slope_grad, NEAR), NEAR).reshape(-1, units)
    branch = lax.dot_general(
        slope_grad,
        up_block,
        (((1,), (1,)), ((), ())),
        preferred_element_type=jnp.float32,
    )
    branch = branch.astype(jnp.bfloat16).reshape(-1, rows, width)
    summed = jnp.sum(exchange(branch, "dp").astype(jnp.float32), axis=0)
    result = (local_grad.astype(jnp.float32) + summed).astype(jnp.bfloat16)
    return result[None]


def solution(mesh):
    sections, dp, tensor = (mesh.shape[a] for a in ("section", "dp", "tensor"))
    fine = Mesh(
        mesh.devices.reshape(sections, dp, tensor // 4, 2, 2),
        ("section", "dp") + TENSOR,
    )
    in_specs = (
        P("section", "dp", TENSOR),
        P("section", TENSOR, "dp"),
        P("section", "dp", TENSOR),
        P("section", ("dp",) + TENSOR, None),
    )
    out_specs = P("section", "dp", TENSOR)
    return jax.shard_map(
        per_device, mesh=fine, in_specs=in_specs, out_specs=out_specs, check_vma=False
    )
```

```python
import jax
import jax.numpy as jnp
from jax import lax
from jax.experimental import pallas as pl
from jax.experimental.pallas import tpu as pltpu
from jax.sharding import Mesh
from jax.sharding import PartitionSpec as P

LONG = pl.CostEstimate(flops=2 * 10**10, bytes_accessed=2**20, transcendentals=0)
TENSOR = ("tx", "ty1", "ty0")
NEAR = ("tx", "ty0")


def exchange(value, axis):
    return lax.all_to_all(value, axis, split_axis=0, concat_axis=0, tiled=True)


def copies(value, axis):
    return jnp.broadcast_to(value[None], (lax.axis_size(axis),) + value.shape)


def shifted(value, axis, steps):
    count = lax.axis_size(axis)
    pairs = [(source, (source + steps) % count) for source in range(count)]
    return lax.ppermute(value, axis, pairs)


def gelu_slope(value):
    coeff = 0.7978845608028654
    inner = coeff * (value + 0.044715 * value * value * value)
    tangent = jnp.tanh(inner)
    return 0.5 * (1.0 + tangent) + 0.5 * value * (1.0 - tangent * tangent) * coeff * (
        1.0 + 3.0 * 0.044715 * value * value
    )


def block_sum(blocks):
    return sum(block.astype(jnp.float32) for block in blocks)


def permuted_blocks(part, axis):
    count, here = lax.axis_size(axis), lax.axis_index(axis)
    blocks = part.reshape((count, part.shape[0] // count) + part.shape[1:])

    def block(steps):
        return lax.dynamic_index_in_dim(
            blocks, (here + steps) % count, axis=0, keepdims=False
        )

    return [block(0)] + [
        shifted(block(steps), axis, steps) for steps in range(1, count)
    ]


def copies_kernel(value_ref, copies_ref, sems):
    moves = [
        pltpu.make_async_copy(value_ref, copies_ref.at[at], sems.at[at])
        for at in range(copies_ref.shape[0])
    ]
    for move in moves:
        move.start()
    for move in moves:
        move.wait()


def long_copies(value, axis):
    count = lax.axis_size(axis)
    return pl.pallas_call(
        copies_kernel,
        out_shape=jax.ShapeDtypeStruct((count,) + value.shape, value.dtype),
        in_specs=[pl.BlockSpec(memory_space=pl.ANY)],
        out_specs=pl.BlockSpec(memory_space=pltpu.HBM),
        scratch_shapes=[pltpu.SemaphoreType.DMA((count,))],
        compiler_params=pltpu.CompilerParams(vmem_limit_bytes=2**20),
        cost_estimate=LONG,
    )(value)


def turned_dot_kernel(left_ref, right_hbm, out_hbm, right_ref, out_ref, sems, out_sems):
    parts, step = right_ref.shape[:2]
    fetches = [
        pltpu.make_async_copy(
            right_hbm.at[pl.ds(at * step, step)], right_ref.at[at], sems.at[at]
        )
        for at in range(parts)
    ]
    stores = [
        pltpu.make_async_copy(
            out_ref.at[at], out_hbm.at[:, pl.ds(at * step, step)], out_sems.at[at]
        )
        for at in range(parts)
    ]
    for fetch in fetches:
        fetch.start()
    for at in range(parts):
        fetches[at].wait()
        out_ref[at] = lax.dot_general(
            left_ref[...],
            right_ref[at],
            (((1,), (1,)), ((), ())),
            preferred_element_type=jnp.float32,
        ).astype(out_ref.dtype)
        stores[at].start()
    for store in stores:
        store.wait()


def turned_dot(left, right):
    parts = 4
    rows, units = left.shape[0], right.shape[0]
    step = units // parts
    return pl.pallas_call(
        turned_dot_kernel,
        out_shape=jax.ShapeDtypeStruct((rows, units), jnp.bfloat16),
        in_specs=[
            pl.BlockSpec(memory_space=pltpu.VMEM),
            pl.BlockSpec(memory_space=pl.ANY),
        ],
        out_specs=pl.BlockSpec(memory_space=pl.ANY),
        scratch_shapes=[
            pltpu.VMEM((parts, step, right.shape[1]), right.dtype),
            pltpu.VMEM((parts, rows, step), jnp.bfloat16),
            pltpu.SemaphoreType.DMA((parts,)),
            pltpu.SemaphoreType.DMA((parts,)),
        ],
        compiler_params=pltpu.CompilerParams(vmem_limit_bytes=8 * 2**20),
        cost_estimate=LONG,
    )(left, pltpu.with_memory_space_constraint(right, pltpu.HBM))


def per_device(saved_input, w_up, w_down, sent_grad):
    tokens_in = saved_input[0]
    up_block = w_up[0]
    down_block = w_down[0]
    rows, width = tokens_in.shape
    near = lax.axis_size(NEAR)
    sent = sent_grad[0]
    parts = lax.axis_size(TENSOR)

    moved = shifted(sent, "section", -1)
    all_tokens = exchange(copies(tokens_in, "dp"), "dp").reshape(-1, width)
    hidden_part = jnp.dot(
        all_tokens, up_block, preferred_element_type=jnp.float32
    ).astype(jnp.bfloat16)
    units = hidden_part.shape[1]

    hidden_part, moved = lax.optimization_barrier((hidden_part, moved))
    moved = moved.reshape(-1, parts, width).transpose(1, 0, 2)
    local_grad = exchange(moved, TENSOR).reshape(rows, width)
    (local_grad,) = lax.optimization_barrier((local_grad,))
    hidden = block_sum(permuted_blocks(hidden_part, "tx")).astype(jnp.bfloat16)
    all_grads = exchange(long_copies(local_grad, "dp"), "dp").reshape(-1, width)
    arrived = permuted_blocks(hidden, "ty0")
    back_part = turned_dot(all_grads, down_block)
    back_part, arrived = lax.optimization_barrier((back_part, arrived))
    hidden = block_sum(arrived).astype(jnp.bfloat16)
    back_near = jnp.sum(
        exchange(back_part.reshape(near, -1, units), NEAR).astype(jnp.float32), axis=0
    ).astype(jnp.bfloat16)
    hidden_far = shifted(hidden, "ty1", 1)
    back_near, hidden_far = lax.optimization_barrier((back_near, hidden_far))
    slope = gelu_slope(block_sum([hidden, hidden_far]))
    back_far = shifted(back_near, "ty1", 1)
    back_far, slope = lax.optimization_barrier((back_far, slope))
    back_hidden = back_near.astype(jnp.float32) + back_far.astype(jnp.float32)
    slope_grad = (back_hidden * slope).astype(jnp.bfloat16)
    slope_grad = exchange(copies(slope_grad, NEAR), NEAR).reshape(-1, units)
    branch = lax.dot_general(
        slope_grad,
        up_block,
        (((1,), (1,)), ((), ())),
        preferred_element_type=jnp.float32,
    )
    branch = branch.astype(jnp.bfloat16).reshape(-1, rows, width)
    summed = jnp.sum(exchange(branch, "dp").astype(jnp.float32), axis=0)
    result = (local_grad.astype(jnp.float32) + summed).astype(jnp.bfloat16)
    return result[None]


def solution(mesh):
    sections, dp, tensor = (mesh.shape[a] for a in ("section", "dp", "tensor"))
    fine = Mesh(
        mesh.devices.reshape(sections, dp, tensor // 4, 2, 2),
        ("section", "dp") + TENSOR,
    )
    in_specs = (
        P("section", "dp", TENSOR),
        P("section", TENSOR, "dp"),
        P("section", "dp", TENSOR),
        P("section", ("dp",) + TENSOR, None),
    )
    out_specs = P("section", "dp", TENSOR)
    return jax.shard_map(
        per_device, mesh=fine, in_specs=in_specs, out_specs=out_specs, check_vma=False
    )
```

```python
import jax
import jax.numpy as jnp
from jax import lax
from jax.experimental import pallas as pl
from jax.experimental.pallas import tpu as pltpu
from jax.sharding import Mesh
from jax.sharding import PartitionSpec as P

LONG = pl.CostEstimate(flops=2 * 10**10, bytes_accessed=2**20, transcendentals=0)
TENSOR = ("tx", "ty1", "ty0")
NEAR = ("tx", "ty0")


def exchange(value, axis):
    return lax.all_to_all(value, axis, split_axis=0, concat_axis=0, tiled=True)


def copies(value, axis):
    return jnp.broadcast_to(value[None], (lax.axis_size(axis),) + value.shape)


def shifted(value, axis, steps):
    count = lax.axis_size(axis)
    pairs = [(source, (source + steps) % count) for source in range(count)]
    return lax.ppermute(value, axis, pairs)


def gelu_slope(value):
    coeff = 0.7978845608028654
    inner = coeff * (value + 0.044715 * value * value * value)
    tangent = jnp.tanh(inner)
    return 0.5 * (1.0 + tangent) + 0.5 * value * (1.0 - tangent * tangent) * coeff * (
        1.0 + 3.0 * 0.044715 * value * value
    )


def block_sum(blocks):
    return sum(block.astype(jnp.float32) for block in blocks)


def permuted_blocks(part, axis):
    count, here = lax.axis_size(axis), lax.axis_index(axis)
    blocks = part.reshape((count, part.shape[0] // count) + part.shape[1:])

    def block(steps):
        return lax.dynamic_index_in_dim(
            blocks, (here + steps) % count, axis=0, keepdims=False
        )

    order = sorted(range(1, count), key=lambda steps: -min(steps, count - steps))
    return [block(0)] + [shifted(block(steps), axis, steps) for steps in order]


def copies_kernel(value_ref, copies_ref, sems):
    moves = [
        pltpu.make_async_copy(value_ref, copies_ref.at[at], sems.at[at])
        for at in range(copies_ref.shape[0])
    ]
    for move in moves:
        move.start()
    for move in moves:
        move.wait()


def long_copies(value, axis):
    count = lax.axis_size(axis)
    return pl.pallas_call(
        copies_kernel,
        out_shape=jax.ShapeDtypeStruct((count,) + value.shape, value.dtype),
        in_specs=[pl.BlockSpec(memory_space=pl.ANY)],
        out_specs=pl.BlockSpec(memory_space=pltpu.HBM),
        scratch_shapes=[pltpu.SemaphoreType.DMA((count,))],
        compiler_params=pltpu.CompilerParams(vmem_limit_bytes=2**20),
        cost_estimate=LONG,
    )(value)


def turned_dot_kernel(left_ref, right_hbm, out_hbm, right_ref, out_ref, sems, out_sems):
    parts, step = right_ref.shape[:2]
    fetches = [
        pltpu.make_async_copy(
            right_hbm.at[pl.ds(at * step, step)], right_ref.at[at], sems.at[at]
        )
        for at in range(parts)
    ]
    stores = [
        pltpu.make_async_copy(
            out_ref.at[at], out_hbm.at[:, pl.ds(at * step, step)], out_sems.at[at]
        )
        for at in range(parts)
    ]
    for fetch in fetches:
        fetch.start()
    for at in range(parts):
        fetches[at].wait()
        out_ref[at] = lax.dot_general(
            left_ref[...],
            right_ref[at],
            (((1,), (1,)), ((), ())),
            preferred_element_type=jnp.float32,
        ).astype(out_ref.dtype)
        stores[at].start()
    for store in stores:
        store.wait()


def turned_dot(left, right):
    parts = 4
    rows, units = left.shape[0], right.shape[0]
    step = units // parts
    return pl.pallas_call(
        turned_dot_kernel,
        out_shape=jax.ShapeDtypeStruct((rows, units), jnp.bfloat16),
        in_specs=[
            pl.BlockSpec(memory_space=pltpu.VMEM),
            pl.BlockSpec(memory_space=pl.ANY),
        ],
        out_specs=pl.BlockSpec(memory_space=pl.ANY),
        scratch_shapes=[
            pltpu.VMEM((parts, step, right.shape[1]), right.dtype),
            pltpu.VMEM((parts, rows, step), jnp.bfloat16),
            pltpu.SemaphoreType.DMA((parts,)),
            pltpu.SemaphoreType.DMA((parts,)),
        ],
        compiler_params=pltpu.CompilerParams(vmem_limit_bytes=8 * 2**20),
        cost_estimate=LONG,
    )(left, pltpu.with_memory_space_constraint(right, pltpu.HBM))


def per_device(saved_input, w_up, w_down, sent_grad):
    tokens_in = saved_input[0]
    up_block = w_up[0]
    down_block = w_down[0]
    rows, width = tokens_in.shape
    near = lax.axis_size(NEAR)
    sent = sent_grad[0]
    parts = lax.axis_size(TENSOR)

    moved = shifted(sent, "section", -1)
    all_tokens = exchange(copies(tokens_in, "dp"), "dp").reshape(-1, width)
    hidden_part = jnp.dot(
        all_tokens, up_block, preferred_element_type=jnp.float32
    ).astype(jnp.bfloat16)
    units = hidden_part.shape[1]

    hidden_part, moved = lax.optimization_barrier((hidden_part, moved))
    moved = moved.reshape(-1, parts, width).transpose(1, 0, 2)
    local_grad = exchange(moved, TENSOR).reshape(rows, width)
    (local_grad,) = lax.optimization_barrier((local_grad,))
    hidden = block_sum(permuted_blocks(hidden_part, "tx")).astype(jnp.bfloat16)
    all_grads = exchange(long_copies(local_grad, "dp"), "dp").reshape(-1, width)
    arrived = permuted_blocks(hidden, "ty0")
    back_part = turned_dot(all_grads, down_block)
    back_part, arrived = lax.optimization_barrier((back_part, arrived))
    hidden = block_sum(arrived).astype(jnp.bfloat16)
    back_near = jnp.sum(
        exchange(back_part.reshape(near, -1, units), NEAR).astype(jnp.float32), axis=0
    ).astype(jnp.bfloat16)
    hidden_far = shifted(hidden, "ty1", 1)
    back_near, hidden_far = lax.optimization_barrier((back_near, hidden_far))
    slope = gelu_slope(block_sum([hidden, hidden_far]))
    back_far = shifted(back_near, "ty1", 1)
    back_far, slope = lax.optimization_barrier((back_far, slope))
    back_hidden = back_near.astype(jnp.float32) + back_far.astype(jnp.float32)
    slope_grad = (back_hidden * slope).astype(jnp.bfloat16)
    slope_grad = exchange(copies(slope_grad, NEAR), NEAR).reshape(-1, units)
    branch = lax.dot_general(
        slope_grad,
        up_block,
        (((1,), (1,)), ((), ())),
        preferred_element_type=jnp.float32,
    )
    branch = branch.astype(jnp.bfloat16).reshape(-1, rows, width)
    summed = jnp.sum(exchange(branch, "dp").astype(jnp.float32), axis=0)
    result = (local_grad.astype(jnp.float32) + summed).astype(jnp.bfloat16)
    return result[None]


def solution(mesh):
    sections, dp, tensor = (mesh.shape[a] for a in ("section", "dp", "tensor"))
    fine = Mesh(
        mesh.devices.reshape(sections, dp, tensor // 4, 2, 2),
        ("section", "dp") + TENSOR,
    )
    in_specs = (
        P("section", "dp", TENSOR),
        P("section", TENSOR, "dp"),
        P("section", "dp", TENSOR),
        P("section", ("dp",) + TENSOR, None),
    )
    out_specs = P("section", "dp", TENSOR)
    return jax.shard_map(
        per_device, mesh=fine, in_specs=in_specs, out_specs=out_specs, check_vma=False
    )
```

```python
import jax
import jax.numpy as jnp
from jax import lax
from jax.experimental import pallas as pl
from jax.experimental.pallas import tpu as pltpu
from jax.sharding import Mesh
from jax.sharding import PartitionSpec as P

LONG = pl.CostEstimate(flops=2 * 10**11, bytes_accessed=2**20, transcendentals=0)
TENSOR = ("tx", "ty1", "ty0")
NEAR = ("tx", "ty0")


def exchange(value, axis):
    return lax.all_to_all(value, axis, split_axis=0, concat_axis=0, tiled=True)


def copies(value, axis):
    return jnp.broadcast_to(value[None], (lax.axis_size(axis),) + value.shape)


def shifted(value, axis, steps):
    count = lax.axis_size(axis)
    pairs = [(source, (source + steps) % count) for source in range(count)]
    return lax.ppermute(value, axis, pairs)


def gelu_slope(value):
    coeff = 0.7978845608028654
    inner = coeff * (value + 0.044715 * value * value * value)
    tangent = jnp.tanh(inner)
    return 0.5 * (1.0 + tangent) + 0.5 * value * (1.0 - tangent * tangent) * coeff * (
        1.0 + 3.0 * 0.044715 * value * value
    )


def block_sum(blocks):
    return sum(block.astype(jnp.float32) for block in blocks)


def permuted_blocks(part, axis):
    count, here = lax.axis_size(axis), lax.axis_index(axis)
    blocks = part.reshape((count, part.shape[0] // count) + part.shape[1:])

    def block(steps):
        return lax.dynamic_index_in_dim(
            blocks, (here + steps) % count, axis=0, keepdims=False
        )

    order = sorted(range(1, count), key=lambda steps: (-min(steps, count - steps), -steps))
    return [block(0)] + [shifted(block(steps), axis, steps) for steps in order]


def copies_kernel(value_ref, copies_ref, sems):
    moves = [
        pltpu.make_async_copy(value_ref, copies_ref.at[at], sems.at[at])
        for at in range(copies_ref.shape[0])
    ]
    for move in moves:
        move.start()
    for move in moves:
        move.wait()


def long_copies(value, axis):
    count = lax.axis_size(axis)
    return pl.pallas_call(
        copies_kernel,
        out_shape=jax.ShapeDtypeStruct((count,) + value.shape, value.dtype),
        in_specs=[pl.BlockSpec(memory_space=pl.ANY)],
        out_specs=pl.BlockSpec(memory_space=pltpu.HBM),
        scratch_shapes=[pltpu.SemaphoreType.DMA((count,))],
        compiler_params=pltpu.CompilerParams(vmem_limit_bytes=2**20),
        cost_estimate=LONG,
    )(value)


def turned_dot_kernel(left_ref, right_hbm, out_hbm, right_ref, out_ref, sems, out_sems):
    parts, step = right_ref.shape[:2]
    fetches = [
        pltpu.make_async_copy(
            right_hbm.at[pl.ds(at * step, step)], right_ref.at[at], sems.at[at]
        )
        for at in range(parts)
    ]
    stores = [
        pltpu.make_async_copy(
            out_ref.at[at], out_hbm.at[:, pl.ds(at * step, step)], out_sems.at[at]
        )
        for at in range(parts)
    ]
    for fetch in fetches:
        fetch.start()
    for at in range(parts):
        fetches[at].wait()
        out_ref[at] = lax.dot_general(
            left_ref[...],
            right_ref[at],
            (((1,), (1,)), ((), ())),
            preferred_element_type=jnp.float32,
        ).astype(out_ref.dtype)
        stores[at].start()
    for store in stores:
        store.wait()


def turned_dot(left, right):
    parts = 4
    rows, units = left.shape[0], right.shape[0]
    step = units // parts
    return pl.pallas_call(
        turned_dot_kernel,
        out_shape=jax.ShapeDtypeStruct((rows, units), jnp.bfloat16),
        in_specs=[
            pl.BlockSpec(memory_space=pltpu.VMEM),
            pl.BlockSpec(memory_space=pl.ANY),
        ],
        out_specs=pl.BlockSpec(memory_space=pl.ANY),
        scratch_shapes=[
            pltpu.VMEM((parts, step, right.shape[1]), right.dtype),
            pltpu.VMEM((parts, rows, step), jnp.bfloat16),
            pltpu.SemaphoreType.DMA((parts,)),
            pltpu.SemaphoreType.DMA((parts,)),
        ],
        compiler_params=pltpu.CompilerParams(vmem_limit_bytes=8 * 2**20),
        cost_estimate=LONG,
    )(left, pltpu.with_memory_space_constraint(right, pltpu.HBM))


def per_device(saved_input, w_up, w_down, sent_grad):
    tokens_in = saved_input[0]
    up_block = w_up[0]
    down_block = w_down[0]
    rows, width = tokens_in.shape
    near = lax.axis_size(NEAR)
    sent = sent_grad[0]
    parts = lax.axis_size(TENSOR)

    moved = shifted(sent, "section", -1)
    all_tokens = exchange(copies(tokens_in, "dp"), "dp").reshape(-1, width)
    hidden_part = jnp.dot(
        all_tokens, up_block, preferred_element_type=jnp.float32
    ).astype(jnp.bfloat16)
    units = hidden_part.shape[1]

    hidden_part, moved = lax.optimization_barrier((hidden_part, moved))
    moved = moved.reshape(-1, parts, width).transpose(1, 0, 2)
    local_grad = exchange(moved, TENSOR).reshape(rows, width)
    (local_grad,) = lax.optimization_barrier((local_grad,))
    hidden = block_sum(permuted_blocks(hidden_part, "tx")).astype(jnp.bfloat16)
    all_grads = exchange(long_copies(local_grad, "dp"), "dp").reshape(-1, width)
    arrived = permuted_blocks(hidden, "ty0")
    back_part = turned_dot(all_grads, down_block)
    back_part, arrived = lax.optimization_barrier((back_part, arrived))
    hidden = block_sum(arrived).astype(jnp.bfloat16)
    back_near = jnp.sum(
        exchange(back_part.reshape(near, -1, units), NEAR).astype(jnp.float32), axis=0
    ).astype(jnp.bfloat16)
    hidden_far = shifted(hidden, "ty1", 1)
    back_near, hidden_far = lax.optimization_barrier((back_near, hidden_far))
    slope = gelu_slope(block_sum([hidden, hidden_far]))
    back_far = shifted(back_near, "ty1", 1)
    back_far, slope = lax.optimization_barrier((back_far, slope))
    back_hidden = back_near.astype(jnp.float32) + back_far.astype(jnp.float32)
    slope_grad = (back_hidden * slope).astype(jnp.bfloat16)
    slope_grad = exchange(copies(slope_grad, NEAR), NEAR).reshape(-1, units)
    branch = lax.dot_general(
        slope_grad,
        up_block,
        (((1,), (1,)), ((), ())),
        preferred_element_type=jnp.float32,
    )
    branch = branch.astype(jnp.bfloat16).reshape(-1, rows, width)
    summed = jnp.sum(exchange(branch, "dp").astype(jnp.float32), axis=0)
    result = (local_grad.astype(jnp.float32) + summed).astype(jnp.bfloat16)
    return result[None]


def solution(mesh):
    sections, dp, tensor = (mesh.shape[a] for a in ("section", "dp", "tensor"))
    fine = Mesh(
        mesh.devices.reshape(sections, dp, tensor // 4, 2, 2),
        ("section", "dp") + TENSOR,
    )
    in_specs = (
        P("section", "dp", TENSOR),
        P("section", TENSOR, "dp"),
        P("section", "dp", TENSOR),
        P("section", ("dp",) + TENSOR, None),
    )
    out_specs = P("section", "dp", TENSOR)
    return jax.shard_map(
        per_device, mesh=fine, in_specs=in_specs, out_specs=out_specs, check_vma=False
    )
```

```python
import jax
import jax.numpy as jnp
from jax import lax
from jax.experimental import pallas as pl
from jax.experimental.pallas import tpu as pltpu
from jax.sharding import Mesh
from jax.sharding import PartitionSpec as P

LONG = pl.CostEstimate(flops=2 * 10**11, bytes_accessed=2**20, transcendentals=0)
TENSOR = ("tx", "ty1", "ty0")
NEAR = ("tx", "ty0")


def exchange(value, axis):
    return lax.all_to_all(value, axis, split_axis=0, concat_axis=0, tiled=True)


def copies(value, axis):
    return jnp.broadcast_to(value[None], (lax.axis_size(axis),) + value.shape)


def shifted(value, axis, steps):
    count = lax.axis_size(axis)
    pairs = [(source, (source + steps) % count) for source in range(count)]
    return lax.ppermute(value, axis, pairs)


def gelu_slope(value):
    coeff = 0.7978845608028654
    inner = coeff * (value + 0.044715 * value * value * value)
    tangent = jnp.tanh(inner)
    return 0.5 * (1.0 + tangent) + 0.5 * value * (1.0 - tangent * tangent) * coeff * (
        1.0 + 3.0 * 0.044715 * value * value
    )


def block_sum(blocks):
    return sum(block.astype(jnp.float32) for block in blocks)


def permuted_blocks(part, axis):
    count, here = lax.axis_size(axis), lax.axis_index(axis)
    blocks = part.reshape((count, part.shape[0] // count) + part.shape[1:])

    def block(steps):
        return lax.dynamic_index_in_dim(
            blocks, (here + steps) % count, axis=0, keepdims=False
        )

    order = sorted(range(1, count), key=lambda steps: (-min(steps, count - steps), -steps))
    return [block(0)] + [shifted(block(steps), axis, steps) for steps in order]


def copies_kernel(value_ref, copies_ref, sems):
    moves = [
        pltpu.make_async_copy(value_ref, copies_ref.at[at], sems.at[at])
        for at in range(copies_ref.shape[0])
    ]
    for move in moves:
        move.start()
    for move in moves:
        move.wait()


def long_copies(value, axis):
    count = lax.axis_size(axis)
    return pl.pallas_call(
        copies_kernel,
        out_shape=jax.ShapeDtypeStruct((count,) + value.shape, value.dtype),
        in_specs=[pl.BlockSpec(memory_space=pl.ANY)],
        out_specs=pl.BlockSpec(memory_space=pltpu.HBM),
        scratch_shapes=[pltpu.SemaphoreType.DMA((count,))],
        compiler_params=pltpu.CompilerParams(vmem_limit_bytes=2**20),
        cost_estimate=LONG,
    )(value)


def turned_dot_kernel(left_ref, right_hbm, out_hbm, right_ref, out_ref, sems, out_sems):
    parts, step = right_ref.shape[:2]
    fetches = [
        pltpu.make_async_copy(
            right_hbm.at[pl.ds(at * step, step)], right_ref.at[at], sems.at[at]
        )
        for at in range(parts)
    ]
    stores = [
        pltpu.make_async_copy(
            out_ref.at[at], out_hbm.at[:, pl.ds(at * step, step)], out_sems.at[at]
        )
        for at in range(parts)
    ]
    for fetch in fetches:
        fetch.start()
    for at in range(parts):
        fetches[at].wait()
        out_ref[at] = lax.dot_general(
            left_ref[...],
            right_ref[at],
            (((1,), (1,)), ((), ())),
            preferred_element_type=jnp.float32,
        ).astype(out_ref.dtype)
        stores[at].start()
    for store in stores:
        store.wait()


def turned_dot(left, right):
    parts = 4
    rows, units = left.shape[0], right.shape[0]
    step = units // parts
    return pl.pallas_call(
        turned_dot_kernel,
        out_shape=jax.ShapeDtypeStruct((rows, units), jnp.bfloat16),
        in_specs=[
            pl.BlockSpec(memory_space=pltpu.VMEM),
            pl.BlockSpec(memory_space=pl.ANY),
        ],
        out_specs=pl.BlockSpec(memory_space=pl.ANY),
        scratch_shapes=[
            pltpu.VMEM((parts, step, right.shape[1]), right.dtype),
            pltpu.VMEM((parts, rows, step), jnp.bfloat16),
            pltpu.SemaphoreType.DMA((parts,)),
            pltpu.SemaphoreType.DMA((parts,)),
        ],
        compiler_params=pltpu.CompilerParams(vmem_limit_bytes=8 * 2**20),
        cost_estimate=LONG,
    )(left, pltpu.with_memory_space_constraint(right, pltpu.HBM))


def per_device(saved_input, w_up, w_down, sent_grad):
    tokens_in = saved_input[0]
    up_block = w_up[0]
    down_block = w_down[0]
    rows, width = tokens_in.shape
    near = lax.axis_size(NEAR)
    sent = sent_grad[0]
    parts = lax.axis_size(TENSOR)

    moved = shifted(sent, "section", -1)
    all_tokens = exchange(copies(tokens_in, "dp"), "dp").reshape(-1, width)
    all_tokens, moved = lax.optimization_barrier((all_tokens, moved))
    hidden_part = jnp.dot(
        all_tokens, up_block, preferred_element_type=jnp.float32
    ).astype(jnp.bfloat16)
    units = hidden_part.shape[1]

    moved = moved.reshape(-1, parts, width).transpose(1, 0, 2)
    local_grad = exchange(moved, TENSOR).reshape(rows, width)
    (local_grad,) = lax.optimization_barrier((local_grad,))
    hidden = block_sum(permuted_blocks(hidden_part, "tx")).astype(jnp.bfloat16)
    all_grads = exchange(long_copies(local_grad, "dp"), "dp").reshape(-1, width)
    arrived = permuted_blocks(hidden, "ty0")
    back_part = turned_dot(all_grads, down_block)
    back_part, arrived = lax.optimization_barrier((back_part, arrived))
    hidden = block_sum(arrived).astype(jnp.bfloat16)
    back_near = jnp.sum(
        exchange(back_part.reshape(near, -1, units), NEAR).astype(jnp.float32), axis=0
    ).astype(jnp.bfloat16)
    hidden_far = shifted(hidden, "ty1", 1)
    back_near, hidden_far = lax.optimization_barrier((back_near, hidden_far))
    slope = gelu_slope(block_sum([hidden, hidden_far]))
    back_far = shifted(back_near, "ty1", 1)
    back_far, slope = lax.optimization_barrier((back_far, slope))
    back_hidden = back_near.astype(jnp.float32) + back_far.astype(jnp.float32)
    slope_grad = (back_hidden * slope).astype(jnp.bfloat16)
    slope_grad = exchange(copies(slope_grad, NEAR), NEAR).reshape(-1, units)
    branch = lax.dot_general(
        slope_grad,
        up_block,
        (((1,), (1,)), ((), ())),
        preferred_element_type=jnp.float32,
    )
    branch = branch.astype(jnp.bfloat16).reshape(-1, rows, width)
    summed = jnp.sum(exchange(branch, "dp").astype(jnp.float32), axis=0)
    result = (local_grad.astype(jnp.float32) + summed).astype(jnp.bfloat16)
    return result[None]


def solution(mesh):
    sections, dp, tensor = (mesh.shape[a] for a in ("section", "dp", "tensor"))
    fine = Mesh(
        mesh.devices.reshape(sections, dp, tensor // 4, 2, 2),
        ("section", "dp") + TENSOR,
    )
    in_specs = (
        P("section", "dp", TENSOR),
        P("section", TENSOR, "dp"),
        P("section", "dp", TENSOR),
        P("section", ("dp",) + TENSOR, None),
    )
    out_specs = P("section", "dp", TENSOR)
    return jax.shard_map(
        per_device, mesh=fine, in_specs=in_specs, out_specs=out_specs, check_vma=False
    )
```
